32 devices in a mesh: island: 4 (over x, core), fsdp: 8 (over z, y).
Axes of the slice: x: 2, y: 2, z: 4, core: 2. Of those that a mesh axis runs over, the one named last changes fastest.
Arguments:
- pseudo_grads: bfloat16 [4, 8192, 1024], P('island', 'fsdp'), as said below
- outer_params: float32 [8192, 1024], P('fsdp'), may hold values from -3 to 3
- momentum: float32 [8192, 1024], P('fsdp'), may hold values from -6 to 6
Outputs:
- new_params: float32 [8192, 1024], P('fsdp')
- new_momentum: float32 [8192, 1024], P('fsdp')
The draws below stay inside these ranges and needn't reach their ends.
Inputs may be any that keep to these rules, and one draw needn't show every extreme that they name: `pseudo_grads`: finite bfloat16 values.
All inputs are finite; a program needn't handle non-finite values.
Results may differ from the reference program's by a relative error of at most 0.0003.
Values sent between devices are 32-bit elements; how exact they have to be, the bound alone decides.
A program may use at most 64 MiB of HBM per device.

```python
import math
import jax
import jax.numpy as jnp
from jax import lax

D = 8192
KV = 1024
ISLANDS = 4


def draw_pseudo_grads(key, part):
    key = jax.random.fold_in(key, 11)
    keys = jax.random.split(key, 4)
    positions = jnp.arange(D, dtype=jnp.float32)
    rising = jnp.exp(jnp.log(3.0) * positions / (D - 1))
    row_scale = rising * jnp.exp(jax.random.uniform(keys[0], (D,)) * jnp.log(10.0))
    col_scale = jnp.exp(jax.random.uniform(keys[1], (KV,)) * jnp.log(10.0))
    island_scale = jnp.exp(jax.random.uniform(keys[2], (ISLANDS, 1, 1)) * jnp.log(3.0))
    noise = jax.random.normal(keys[3], (ISLANDS, D, KV))
    values = 0.05 * island_scale * row_scale[None, :, None] * col_scale[None, None, :] * noise
    return values.astype(jnp.bfloat16)


def level_of(stream_key, shape, cuts, least, largest):
    level = 1.0
    for dim, blocks in cuts:
        heights = jax.random.uniform(jax.random.fold_in(jax.random.fold_in(stream_key, 6), dim), (blocks,), jnp.float32, least / len(cuts), largest / len(cuts))
        level = level * jnp.repeat(jnp.exp(heights), shape[dim] // blocks).reshape((-1,) + (1,) * (len(shape) - 1 - dim))
    return level


def normal_values(stream_key, dims, width, reach, pieces=(), kind=jnp.bfloat16):
    factor_of = level_of(stream_key, dims, pieces, -0.22, 0.18) if pieces else 1.0
    array = jax.random.normal(stream_key, dims, jnp.float32) * width * factor_of
    return jnp.minimum(jnp.maximum(array, -reach), reach).astype(kind)


def setup_inputs(seed: int = 0) -> dict:
    key_of = jax.random.split(jax.random.key(seed), 4)
    return {
        "pseudo_grads": draw_pseudo_grads(jax.random.fold_in(key_of[3], 71), 0),
        "outer_params": normal_values(key_of[1], (D, KV), 0.5, 3.0, ((0, 8),), jnp.float32),
        "momentum": normal_values(key_of[2], (D, KV), 1.0, 6.0, ((0, 8),), jnp.float32),
    }


def reference(pseudo_grads, outer_params, momentum):
    total = lax.optimization_barrier(jnp.sum(pseudo_grads.astype(jnp.float32), axis=0))
    average = total / ISLANDS
    squares = jnp.sum(average * average)
    threshold = 0.2 * math.sqrt(D * KV)
    factor = jnp.minimum(1.0, threshold / jnp.sqrt(squares + 1e-06))
    clipped = factor * average
    new_momentum = 0.9 * momentum + clipped
    new_params = outer_params - 0.7 * (clipped + 0.9 * new_momentum)
    return (new_params, new_momentum)
```

```python
import functools
import math

import jax
import jax.numpy as jnp
from jax import lax
from jax.experimental import pallas as pl
from jax.experimental.pallas import tpu as pltpu
from jax.sharding import PartitionSpec as P

MESH = pl.DeviceIdType.MESH
CORES = 2


def fold(block):
    total = None
    for r in range(0, block.shape[0], 8):
        for c in range(0, block.shape[1], 128):
            tile = block[r : r + 8, c : c + 128]
            total = tile if total is None else total + tile
    return total


def kernel(
    chips, groups, chunk, grads, average, squares,
    local, staged, paired, outgoing, arrived, pair_sums, chip_sums, group_sums,
    load_sem, pair_send, pair_recv, part_send, part_recv, full_send, full_recv,
    share_send, share_recv, sum_send, sum_recv,
):
    rows, cols = average.shape
    half = rows // CORES
    piece = half // chips
    count = piece // chunk
    island = lax.axis_index("island")
    group = lax.axis_index("fsdp")
    chip, core = lax.div(island, CORES), lax.rem(island, CORES)
    other = 1 - core
    sibling = {"island": chip * CORES + other}

    def owner(p):
        return lax.rem(chip + p, chips)

    def peer(p):
        return {"island": owner(p) * CORES + core}

    def start_of(which_core, p, j):
        return pl.multiple_of(which_core * half + owner(p) * piece + j * chunk, chunk)

    def span(j):
        return pl.ds(pl.multiple_of(j * chunk, chunk), chunk)

    barrier = pltpu.get_barrier_semaphore()
    pl.semaphore_signal(barrier, inc=1, device_id=sibling, device_id_type=MESH)
    for p in range(1, chips):
        pl.semaphore_signal(barrier, inc=1, device_id=peer(p), device_id_type=MESH)
    for s in range(1, groups):
        pl.semaphore_signal(
            barrier, inc=1, device_id={"fsdp": lax.rem(group + s, groups)}, device_id_type=MESH
        )

    def load(side, p):
        which = other if side == 0 else core
        place = pl.ds(start_of(which, p, 0), piece)
        return pltpu.make_async_copy(
            grads.at[0, place], local.at[place], load_sem.at[side, p]
        )

    order = [*range(1, chips), 0]
    for p in order:
        load(0, p).start()
        load(1, p).start()

    def to_sibling(p, j):
        return pltpu.make_async_remote_copy(
            staged.at[p, span(j)], paired.at[p, span(j)],
            pair_send.at[p, j], pair_recv.at[p, j], sibling, MESH,
        )

    def part_to_peer(p, j, back):
        slot = (chips - p if back else p) - 1
        return pltpu.make_async_remote_copy(
            outgoing.at[p - 1, span(j)], arrived.at[slot, span(j)],
            part_send.at[p - 1, j], part_recv.at[slot, j], peer(p), MESH,
        )

    def full_to_peer(p, j, whose, slot):
        place = pl.ds(start_of(core, whose, j), chunk)
        return pltpu.make_async_remote_copy(
            average.at[place], average.at[place],
            full_send.at[p - 1, j], full_recv.at[slot - 1, j], peer(p), MESH,
        )

    def full_to_sibling(p, j, which):
        place = pl.ds(start_of(which, p, j), chunk)
        return pltpu.make_async_remote_copy(
            average.at[place], average.at[place],
            share_send.at[p, j], share_recv.at[p, j], sibling, MESH,
        )

    def each(body):
        lax.fori_loop(0, count, lambda j, _: body(j), None)

    def send_pair(p):
        load(0, p).wait()

        def body(j):
            block = local[pl.ds(start_of(other, p, j), chunk)]
            staged[p, span(j)] = block.astype(jnp.float32)
            to_sibling(p, j).start()

        each(body)

    def chip_sum(p, j):
        to_sibling(p, j).wait_recv()
        mine = local[pl.ds(start_of(core, p, j), chunk)].astype(jnp.float32)
        return mine + paired[p, span(j)]

    pl.semaphore_wait(barrier, 1 + (chips - 1) + (groups - 1))
    for p in range(1, chips):
        send_pair(p)
    for p in range(1, chips):
        load(1, p).wait()

        def send_part(j, p=p):
            outgoing[p - 1, span(j)] = chip_sum(p, j)
            part_to_peer(p, j, True).start()

        each(send_part)
    send_pair(0)
    load(1, 0).wait()

    def finish(j, partial):
        total = chip_sum(0, j)
        for p in range(1, chips):
            part_to_peer(p, j, False).wait_recv()
            total = total + arrived[p - 1, span(j)]
        mean = total / (chips * CORES)
        average[pl.ds(start_of(core, 0, j), chunk)] = mean
        for p in range(1, chips):
            full_to_peer(p, j, 0, chips - p).start()
        full_to_sibling(0, j, core).start()
        return partial + fold(mean * mean)

    partial = lax.fori_loop(0, count, finish, jnp.zeros((8, 128), jnp.float32))

    def exchange(slots, mine, value, targets, first):
        slots[mine] = value
        copies = []
        for s, target in enumerate(targets):
            copy = pltpu.make_async_remote_copy(
                slots.at[mine], slots.at[mine],
                sum_send.at[first + s], sum_recv.at[first + s], target, MESH,
            )
            copy.start()
            copies.append(copy)
        for copy in copies:
            copy.wait_recv()
        total = slots[0]
        for s in range(1, slots.shape[0]):
            total = total + slots[s]
        return total, copies

    total, sent_a = exchange(pair_sums, core, partial, [sibling], 0)
    total, sent_b = exchange(chip_sums, chip, total, [peer(p) for p in range(1, chips)], 1)
    total, sent_c = exchange(
        group_sums, group, total,
        [{"fsdp": lax.rem(group + s, groups)} for s in range(1, groups)], chips,
    )
    squares[...] = jnp.broadcast_to(jnp.sum(total), squares.shape)

    def forward(j):
        for p in range(1, chips):
            full_to_peer(p, j, p, p).wait_recv()
            full_to_sibling(p, j, core).start()

    each(forward)

    def close(j):
        for p in range(chips):
            full_to_sibling(p, j, other).wait_recv()
            full_to_sibling(p, j, core).wait_send()
            to_sibling(p, j).wait_send()
        for p in range(1, chips):
            part_to_peer(p, j, True).wait_send()
            full_to_peer(p, j, 0, p).wait_send()

    each(close)
    for copy in sent_a + sent_b + sent_c:
        copy.wait_send()


def mean_and_squares(grads, islands, groups):
    rows, cols = grads.shape[1:]
    chips = islands // CORES
    piece = rows // islands
    chunk = max(16, piece // 8)
    count = piece // chunk
    wide = jnp.float32
    dma = pltpu.SemaphoreType.DMA
    return pl.pallas_call(
        functools.partial(kernel, chips, groups, chunk),
        out_shape=[
            jax.ShapeDtypeStruct((rows, cols), wide),
            jax.ShapeDtypeStruct((8, 128), wide),
        ],
        in_specs=[pl.BlockSpec(memory_space=pl.ANY)],
        out_specs=[pl.BlockSpec(memory_space=pltpu.VMEM)] * 2,
        scratch_shapes=[
            pltpu.VMEM((rows, cols), grads.dtype),
            pltpu.VMEM((chips, piece, cols), wide),
            pltpu.VMEM((chips, piece, cols), wide),
            pltpu.VMEM((max(chips - 1, 1), piece, cols), wide),
            pltpu.VMEM((max(chips - 1, 1), piece, cols), wide),
            pltpu.VMEM((CORES, 8, 128), wide),
            pltpu.VMEM((chips, 8, 128), wide),
            pltpu.VMEM((groups, 8, 128), wide),
            dma((2, chips)),
            dma((chips, count)),
            dma((chips, count)),
            dma((chips - 1, count)),
            dma((chips - 1, count)),
            dma((chips - 1, count)),
            dma((chips - 1, count)),
            dma((chips, count)),
            dma((chips, count)),
            dma((chips + groups - 1,)),
            dma((chips + groups - 1,)),
        ],
        compiler_params=pltpu.CompilerParams(
            collective_id=0, has_side_effects=True, vmem_limit_bytes=24 * 2**20
        ),
        cost_estimate=pl.CostEstimate(
            flops=8 * rows * cols, bytes_accessed=6 * rows * cols, transcendentals=0
        ),
    )(grads)


def per_device(pseudo_grads, outer_params, momentum):
    rows, cols = outer_params.shape
    groups = lax.axis_size("fsdp")
    average, sums = mean_and_squares(pseudo_grads, lax.axis_size("island"), groups)
    squares = sums[0, 0]
    threshold = 0.2 * math.sqrt(rows * groups * cols)
    factor = jnp.minimum(1.0, threshold / jnp.sqrt(squares + 1e-06))
    clipped = factor * average
    moment_next = 0.9 * momentum + clipped
    params_next = outer_params - 0.7 * (clipped + 0.9 * moment_next)
    return params_next, moment_next


def solution(mesh):
    return jax.shard_map(
        per_device,
        mesh=mesh,
        in_specs=(P("island", "fsdp", None), P("fsdp", None), P("fsdp", None)),
        out_specs=(P("fsdp", None), P("fsdp", None)),
        check_vma=False,
    )
```

```python
import functools
import math

import jax
import jax.numpy as jnp
from jax import lax
from jax.experimental import pallas as pl
from jax.experimental.pallas import tpu as pltpu
from jax.sharding import PartitionSpec as P

MESH = pl.DeviceIdType.MESH
CORES = 2
CHUNKS = 8
AHEAD = 2


def fold(block):
    total = None
    for r in range(0, block.shape[0], 8):
        for c in range(0, block.shape[1], 128):
            tile = block[r : r + 8, c : c + 128]
            total = tile if total is None else total + tile
    return total


def kernel(
    chips, groups, chunk, threshold, grads, outer, moment, params_out, moment_out,
    average, local, staged, paired, outgoing, arrived, pair_sums, chip_sums, group_sums,
    load_sem, state_sem, pair_send, pair_recv, part_send, part_recv, full_send, full_recv,
    share_send, share_recv, sum_send, sum_recv,
):
    rows, cols = average.shape
    half = rows // CORES
    piece = half // chips
    count = piece // chunk
    island = lax.axis_index("island")
    group = lax.axis_index("fsdp")
    chip, core = lax.div(island, CORES), lax.rem(island, CORES)
    other = 1 - core
    sibling = {"island": chip * CORES + other}

    def owner(p):
        return lax.rem(chip + p, chips)

    def peer(p):
        return {"island": owner(p) * CORES + core}

    def start_of(which_core, p, j):
        return pl.multiple_of(which_core * half + owner(p) * piece + j * chunk, chunk)

    def span(j):
        return pl.ds(pl.multiple_of(j * chunk, chunk), chunk)

    barrier = pltpu.get_barrier_semaphore()
    pl.semaphore_signal(barrier, inc=1, device_id=sibling, device_id_type=MESH)
    for p in range(1, chips):
        pl.semaphore_signal(barrier, inc=1, device_id=peer(p), device_id_type=MESH)
    for s in range(1, groups):
        pl.semaphore_signal(
            barrier, inc=1, device_id={"fsdp": lax.rem(group + s, groups)}, device_id_type=MESH
        )

    def load(side, p):
        which = other if side == 0 else core
        place = pl.ds(start_of(which, p, 0), piece)
        return pltpu.make_async_copy(
            grads.at[0, place], local.at[place], load_sem.at[side, p]
        )

    order = [*range(1, chips), 0]
    for p in order:
        load(0, p).start()
        load(1, p).start()

    state = [
        pltpu.make_async_copy(outer, params_out, state_sem.at[0]),
        pltpu.make_async_copy(moment, moment_out, state_sem.at[1]),
    ]

    def to_sibling(p, j):
        return pltpu.make_async_remote_copy(
            staged.at[p, span(j)], paired.at[p, span(j)],
            pair_send.at[p, j], pair_recv.at[p, j], sibling, MESH,
        )

    def part_to_peer(p, j, back):
        slot = (chips - p if back else p) - 1
        return pltpu.make_async_remote_copy(
            outgoing.at[p - 1, span(j)], arrived.at[slot, span(j)],
            part_send.at[p - 1, j], part_recv.at[slot, j], peer(p), MESH,
        )

    def full_to_peer(p, j, whose, slot):
        place = pl.ds(start_of(core, whose, j), chunk)
        return pltpu.make_async_remote_copy(
            average.at[place], average.at[place],
            full_send.at[p - 1, j], full_recv.at[slot - 1, j], peer(p), MESH,
        )

    def full_to_sibling(p, j, which):
        place = pl.ds(start_of(which, p, j), chunk)
        return pltpu.make_async_remote_copy(
            average.at[place], average.at[place],
            share_send.at[p, j], share_recv.at[p, j], sibling, MESH,
        )

    def each(body):
        lax.fori_loop(0, count, lambda j, _: body(j), None)

    def send_pair(p):
        load(0, p).wait()

        def body(j):
            block = local[pl.ds(start_of(other, p, j), chunk)]
            staged[p, span(j)] = block.astype(jnp.float32)
            to_sibling(p, j).start()

        each(body)

    def chip_sum(p, j):
        to_sibling(p, j).wait_recv()
        mine = local[pl.ds(start_of(core, p, j), chunk)].astype(jnp.float32)
        return mine + paired[p, span(j)]

    pl.semaphore_wait(barrier, 1 + (chips - 1) + (groups - 1))
    for p in range(1, chips):
        send_pair(p)
    for p in range(1, chips):
        load(1, p).wait()

        def send_part(j, p=p):
            outgoing[p - 1, span(j)] = chip_sum(p, j)
            part_to_peer(p, j, True).start()

        each(send_part)
    send_pair(0)
    load(1, 0).wait()
    for copy in state:
        copy.start()

    def gather(j):
        for p in range(1, chips):
            full_to_peer(p, j, 0, chips - p).start()

    def finish(j, partial):
        total = chip_sum(0, j)
        for p in range(1, chips):
            part_to_peer(p, j, False).wait_recv()
            total = total + arrived[p - 1, span(j)]
        mean = total / (chips * CORES)
        average[pl.ds(start_of(core, 0, j), chunk)] = mean
        pl.when(j < AHEAD)(lambda: gather(j))
        full_to_sibling(0, j, core).start()
        return partial + fold(mean * mean)

    partial = lax.fori_loop(0, count, finish, jnp.zeros((8, 128), jnp.float32))

    def send_sum(slots, mine, value, targets, first):
        slots[mine] = value
        copies = []
        for s, target in enumerate(targets):
            copy = pltpu.make_async_remote_copy(
                slots.at[mine], slots.at[mine],
                sum_send.at[first + s], sum_recv.at[first + s], target, MESH,
            )
            copy.start()
            copies.append(copy)
        return copies

    def take_sum(slots, copies):
        for copy in copies:
            copy.wait_recv()
        total = slots[0]
        for s in range(1, slots.shape[0]):
            total = total + slots[s]
        return total

    sent_a = send_sum(chip_sums, chip, partial, [peer(p) for p in range(1, chips)], 1)

    def gather_rest(j, _):
        gather(j)

    lax.fori_loop(min(AHEAD, count), count, gather_rest, None)
    total = take_sum(chip_sums, sent_a)
    sent_b = send_sum(pair_sums, core, total, [sibling], 0)
    total = take_sum(pair_sums, sent_b)
    sent_c = send_sum(
        group_sums, group, total,
        [{"fsdp": lax.rem(group + s, groups)} for s in range(1, groups)], chips,
    )
    squares = jnp.sum(take_sum(group_sums, sent_c), keepdims=True)
    factor = jnp.minimum(1.0, threshold / jnp.sqrt(squares + 1e-06))
    for copy in state:
        copy.wait()

    def update(which, p, j):
        place = pl.ds(start_of(which, p, j), chunk)
        clipped = factor * average[place]
        moment_next = 0.9 * moment_out[place] + clipped
        moment_out[place] = moment_next
        params_out[place] = params_out[place] - 0.7 * (clipped + 0.9 * moment_next)

    def own(j):
        update(core, 0, j)
        full_to_sibling(0, j, other).wait_recv()
        update(other, 0, j)

    each(own)

    def from_sibling(j):
        for p in range(1, chips):
            full_to_sibling(p, j, other).wait_recv()
            update(other, p, j)

    def forward(j):
        for p in range(1, chips):
            full_to_peer(p, j, p, p).wait_recv()
            full_to_sibling(p, j, core).start()
        for p in range(1, chips):
            update(core, p, j)
        pl.when(j > 0)(lambda: from_sibling(j - 1))

    each(forward)
    from_sibling(count - 1)

    def close(j):
        for p in range(chips):
            full_to_sibling(p, j, core).wait_send()
            to_sibling(p, j).wait_send()
        for p in range(1, chips):
            part_to_peer(p, j, True).wait_send()
            full_to_peer(p, j, 0, p).wait_send()

    each(close)
    for copy in sent_a + sent_b + sent_c:
        copy.wait_send()


def step(islands, groups, grads, outer, moment):
    rows, cols = outer.shape
    chips = islands // CORES
    piece = rows // islands
    chunk = max(16, piece // CHUNKS)
    count = piece // chunk
    threshold = 0.2 * math.sqrt(rows * groups * cols)
    wide = jnp.float32
    dma = pltpu.SemaphoreType.DMA
    return pl.pallas_call(
        functools.partial(kernel, chips, groups, chunk, threshold),
        out_shape=[pltpu.VMEM((rows, cols), wide)] * 2,
        in_specs=[pl.BlockSpec(memory_space=pltpu.HBM)] * 3,
        out_specs=[pl.BlockSpec(memory_space=pltpu.VMEM)] * 2,
        scratch_shapes=[
            pltpu.VMEM((rows, cols), wide),
            pltpu.VMEM((rows, cols), grads.dtype),
            pltpu.VMEM((chips, piece, cols), wide),
            pltpu.VMEM((chips, piece, cols), wide),
            pltpu.VMEM((max(chips - 1, 1), piece, cols), wide),
            pltpu.VMEM((max(chips - 1, 1), piece, cols), wide),
            pltpu.VMEM((CORES, 8, 128), wide),
            pltpu.VMEM((chips, 8, 128), wide),
            pltpu.VMEM((groups, 8, 128), wide),
            dma((2, chips)),
            dma((2,)),
            dma((chips, count)),
            dma((chips, count)),
            dma((chips - 1, count)),
            dma((chips - 1, count)),
            dma((chips - 1, count)),
            dma((chips - 1, count)),
            dma((chips, count)),
            dma((chips, count)),
            dma((chips + groups - 1,)),
            dma((chips + groups - 1,)),
        ],
        compiler_params=pltpu.CompilerParams(
            collective_id=0, has_side_effects=True, vmem_limit_bytes=32 * 2**20
        ),
        cost_estimate=pl.CostEstimate(
            flops=16 * rows * cols, bytes_accessed=10 * rows * cols, transcendentals=0
        ),
    )(*(pltpu.with_memory_space_constraint(x, pltpu.HBM) for x in (grads, outer, moment)))


def per_device(pseudo_grads, outer_params, momentum):
    islands, groups = lax.axis_size("island"), lax.axis_size("fsdp")
    return tuple(step(islands, groups, pseudo_grads, outer_params, momentum))


def solution(mesh):
    return jax.shard_map(
        per_device,
        mesh=mesh,
        in_specs=(P("island", "fsdp", None), P("fsdp", None), P("fsdp", None)),
        out_specs=(P("fsdp", None), P("fsdp", None)),
        check_vma=False,
    )
```

```python
import functools
import math

import jax
import jax.numpy as jnp
from jax import lax
from jax.experimental import pallas as pl
from jax.experimental.pallas import tpu as pltpu
from jax.sharding import PartitionSpec as P

MESH = pl.DeviceIdType.MESH
CORES = 2
CHUNKS = 8
AHEAD = 2
STORES = 4


def fold(block):
    total = None
    for r in range(0, block.shape[0], 8):
        for c in range(0, block.shape[1], 128):
            tile = block[r : r + 8, c : c + 128]
            total = tile if total is None else total + tile
    return total


def kernel(
    chips, groups, chunk, threshold, grads, outer, moment, params_out, moment_out,
    average, local, staged, paired, outgoing, arrived, pair_sums, chip_sums, group_sums, total_sum,
    load_sem, state_sem, pair_send, pair_recv, part_send, part_recv, full_send, full_recv,
    share_send, share_recv, sum_send, sum_recv, ready,
):
    rows, cols = average.shape
    half = rows // CORES
    piece = half // chips
    count = piece // chunk
    island = lax.axis_index("island")
    group = lax.axis_index("fsdp")
    chip, core = lax.div(island, CORES), lax.rem(island, CORES)
    other = 1 - core
    sibling = {"island": chip * CORES + other}

    def owner(p):
        return lax.rem(chip + p, chips)

    def peer(p):
        return {"island": owner(p) * CORES + core}

    def start_of(which_core, p, j):
        return pl.multiple_of(which_core * half + owner(p) * piece + j * chunk, chunk)

    def span(j):
        return pl.ds(pl.multiple_of(j * chunk, chunk), chunk)

    barrier = pltpu.get_barrier_semaphore()
    lead = core == 0
    mates = [{"fsdp": lax.rem(group + s, groups)} for s in range(1, groups)]

    @pl.when(lead)
    def _():
        for p in range(chips):
            pl.semaphore_signal(
                barrier, inc=1, device_id={"island": owner(p) * CORES + 1}, device_id_type=MESH
            )
        for mate in mates:
            pl.semaphore_signal(barrier, inc=1, device_id=mate, device_id_type=MESH)

    @pl.when(jnp.logical_not(lead))
    def _():
        for p in range(1, chips):
            pl.semaphore_signal(barrier, inc=1, device_id=peer(p), device_id_type=MESH)

    def load(side, p):
        which = other if side == 0 else core
        place = pl.ds(start_of(which, p, 0), piece)
        return pltpu.make_async_copy(
            grads.at[0, place], local.at[place], load_sem.at[side, p]
        )

    order = [*range(1, chips), 0]
    for p in order:
        load(0, p).start()
        load(1, p).start()

    state = [
        pltpu.make_async_copy(outer, params_out, state_sem.at[0]),
        pltpu.make_async_copy(moment, moment_out, state_sem.at[1]),
    ]

    def to_sibling(p, j):
        return pltpu.make_async_remote_copy(
            staged.at[p, span(j)], paired.at[p, span(j)],
            pair_send.at[p, j], pair_recv.at[p, j], sibling, MESH,
        )

    def part_to_peer(p, j, back):
        slot = (chips - p if back else p) - 1
        return pltpu.make_async_remote_copy(
            outgoing.at[p - 1, span(j)], arrived.at[slot, span(j)],
            part_send.at[p - 1, j], part_recv.at[slot, j], peer(p), MESH,
        )

    def full_to_peer(p, j, whose, slot):
        place = pl.ds(start_of(core, whose, j), chunk)
        return pltpu.make_async_remote_copy(
            average.at[place], average.at[place],
            full_send.at[p - 1, j], full_recv.at[slot - 1, j], peer(p), MESH,
        )

    def full_to_sibling(p, j, which):
        place = pl.ds(start_of(which, p, j), chunk)
        return pltpu.make_async_remote_copy(
            average.at[place], average.at[place],
            share_send.at[p, j], share_recv.at[p, j], sibling, MESH,
        )

    def each(body):
        lax.fori_loop(0, count, lambda j, _: body(j), None)

    def send_pair(p):
        load(0, p).wait()

        def body(j):
            block = local[pl.ds(start_of(other, p, j), chunk)]
            staged[p, span(j)] = block.astype(jnp.float32)
            to_sibling(p, j).start()

        each(body)

    def chip_sum(p, j):
        to_sibling(p, j).wait_recv()
        mine = local[pl.ds(start_of(core, p, j), chunk)].astype(jnp.float32)
        return mine + paired[p, span(j)]

    @pl.when(jnp.logical_not(lead))
    def _():
        pl.semaphore_wait(barrier, chips + (chips - 1))
        pl.semaphore_signal(ready, inc=1, device_id=sibling, device_id_type=MESH)

    @pl.when(lead)
    def _():
        pl.semaphore_wait(ready, 1)

    for p in range(1, chips):
        send_pair(p)
    for p in range(1, chips):
        load(1, p).wait()

        def send_part(j, p=p):
            outgoing[p - 1, span(j)] = chip_sum(p, j)
            part_to_peer(p, j, True).start()

        each(send_part)
    send_pair(0)
    load(1, 0).wait()
    for copy in state:
        copy.start()

    def gather(j):
        for p in range(1, chips):
            full_to_peer(p, j, 0, chips - p).start()

    def finish(j, partial):
        total = chip_sum(0, j)
        for p in range(1, chips):
            part_to_peer(p, j, False).wait_recv()
            total = total + arrived[p - 1, span(j)]
        mean = total / (chips * CORES)
        average[pl.ds(start_of(core, 0, j), chunk)] = mean
        pl.when(j < AHEAD)(lambda: gather(j))
        full_to_sibling(0, j, core).start()
        return partial + fold(mean * mean)

    partial = lax.fori_loop(0, count, finish, jnp.zeros((8, 128), jnp.float32))

    def sum_copy(slots, mine, number, target):
        return pltpu.make_async_remote_copy(
            slots.at[mine], slots.at[mine],
            sum_send.at[number], sum_recv.at[number], target, MESH,
        )

    def send_sums(slots, mine, value, targets, first):
        slots[mine] = value
        copies = [sum_copy(slots, mine, first + s, t) for s, t in enumerate(targets)]
        for copy in copies:
            copy.start()
        return copies

    def add_up(slots):
        total = slots[0]
        for s in range(1, slots.shape[0]):
            total = total + slots[s]
        return total

    sent = send_sums(chip_sums, chip, partial, [peer(p) for p in range(1, chips)], 2)

    def gather_rest(j, _):
        gather(j)

    lax.fori_loop(min(AHEAD, count), count, gather_rest, None)
    for copy in sent:
        copy.wait_recv()
    pair_sums[core] = add_up(chip_sums)
    from_pair = sum_copy(pair_sums, 1, 0, sibling)
    whole = sum_copy(total_sum, 0, 1, sibling)

    @pl.when(jnp.logical_not(lead))
    def _():
        from_pair.start()
        whole.wait_recv()
        from_pair.wait_send()

    @pl.when(lead)
    def _():
        pl.semaphore_wait(barrier, groups - 1)
        from_pair.wait_recv()
        copies = send_sums(group_sums, group, add_up(pair_sums), mates, 1 + chips)
        for copy in copies:
            copy.wait_recv()
        total_sum[0] = add_up(group_sums)
        whole.start()
        for copy in copies:
            copy.wait_send()
        whole.wait_send()

    squares = jnp.sum(total_sum[0], keepdims=True)
    factor = jnp.minimum(1.0, threshold / jnp.sqrt(squares + 1e-06))
    for copy in state:
        copy.wait()

    def update(which, p, j):
        place = pl.ds(start_of(which, p, j), chunk)
        clipped = factor * average[place]
        moment_next = 0.9 * moment_out[place] + clipped
        moment_out[place] = moment_next
        params_out[place] = params_out[place] - 0.7 * (clipped + 0.9 * moment_next)

    def own(j):
        update(core, 0, j)
        full_to_sibling(0, j, other).wait_recv()
        update(other, 0, j)

    each(own)

    def from_sibling(j):
        for p in range(1, chips):
            full_to_sibling(p, j, other).wait_recv()
            update(other, p, j)

    def forward(j):
        for p in range(1, chips):
            full_to_peer(p, j, p, p).wait_recv()
            full_to_sibling(p, j, core).start()
        for p in range(1, chips):
            update(core, p, j)
        pl.when(j > 0)(lambda: from_sibling(j - 1))

    each(forward)
    from_sibling(count - 1)

    def close(j):
        for p in range(chips):
            full_to_sibling(p, j, core).wait_send()
            to_sibling(p, j).wait_send()
        for p in range(1, chips):
            part_to_peer(p, j, True).wait_send()
            full_to_peer(p, j, 0, p).wait_send()

    each(close)
    for copy in sent:
        copy.wait_send()


def step(islands, groups, grads, outer, moment):
    rows, cols = outer.shape
    chips = islands // CORES
    piece = rows // islands
    chunk = max(16, piece // CHUNKS)
    count = piece // chunk
    threshold = 0.2 * math.sqrt(rows * groups * cols)
    wide = jnp.float32
    dma = pltpu.SemaphoreType.DMA
    return pl.pallas_call(
        functools.partial(kernel, chips, groups, chunk, threshold),
        out_shape=[pltpu.VMEM((rows, cols), wide)] * 2,
        in_specs=[pl.BlockSpec(memory_space=pltpu.HBM)] * 3,
        out_specs=[pl.BlockSpec(memory_space=pltpu.VMEM)] * 2,
        scratch_shapes=[
            pltpu.VMEM((rows, cols), wide),
            pltpu.VMEM((rows, cols), grads.dtype),
            pltpu.VMEM((chips, piece, cols), wide),
            pltpu.VMEM((chips, piece, cols), wide),
            pltpu.VMEM((max(chips - 1, 1), piece, cols), wide),
            pltpu.VMEM((max(chips - 1, 1), piece, cols), wide),
            pltpu.VMEM((CORES, 8, 128), wide),
            pltpu.VMEM((chips, 8, 128), wide),
            pltpu.VMEM((groups, 8, 128), wide),
            pltpu.VMEM((1, 8, 128), wide),
            dma((2, chips)),
            dma((2,)),
            dma((chips, count)),
            dma((chips, count)),
            dma((chips - 1, count)),
            dma((chips - 1, count)),
            dma((chips - 1, count)),
            dma((chips - 1, count)),
            dma((chips, count)),
            dma((chips, count)),
            dma((chips + groups,)),
            dma((chips + groups,)),
            pltpu.SemaphoreType.REGULAR,
        ],
        compiler_params=pltpu.CompilerParams(
            collective_id=0, has_side_effects=True, vmem_limit_bytes=32 * 2**20
        ),
        cost_estimate=pl.CostEstimate(
            flops=16 * rows * cols, bytes_accessed=10 * rows * cols, transcendentals=0
        ),
    )(*(pltpu.with_memory_space_constraint(x, pltpu.HBM) for x in (grads, outer, moment)))


def store_kernel(params, moment, params_out, moment_out, sem):
    part = params.shape[0] // STORES
    copies = []
    for s in range(STORES):
        place = pl.ds(s * part, part)
        for a, (source, target) in enumerate([(params, params_out), (moment, moment_out)]):
            copies.append(pltpu.make_async_copy(source.at[place], target.at[place], sem.at[a, s]))
    for copy in copies:
        copy.start()
    for copy in copies:
        copy.wait()


def store(results):
    return pl.pallas_call(
        store_kernel,
        out_shape=[jax.ShapeDtypeStruct(x.shape, x.dtype) for x in results],
        in_specs=[pl.BlockSpec(memory_space=pltpu.VMEM)] * 2,
        out_specs=[pl.BlockSpec(memory_space=pltpu.HBM)] * 2,
        scratch_shapes=[pltpu.SemaphoreType.DMA((2, STORES))],
        compiler_params=pltpu.CompilerParams(vmem_limit_bytes=4 * 2**20),
    )(*(pltpu.with_memory_space_constraint(x, pltpu.VMEM) for x in results))


def per_device(pseudo_grads, outer_params, momentum):
    islands, groups = lax.axis_size("island"), lax.axis_size("fsdp")
    return tuple(store(step(islands, groups, pseudo_grads, outer_params, momentum)))


def solution(mesh):
    return jax.shard_map(
        per_device,
        mesh=mesh,
        in_specs=(P("island", "fsdp", None), P("fsdp", None), P("fsdp", None)),
        out_specs=(P("fsdp", None), P("fsdp", None)),
        check_vma=False,
    )
```

```python
import functools
import math

import jax
import jax.numpy as jnp
from jax import lax
from jax.experimental import pallas as pl
from jax.experimental.pallas import tpu as pltpu
from jax.sharding import PartitionSpec as P

MESH = pl.DeviceIdType.MESH
CORES = 2
CHUNKS = 4
AHEAD = 2
STORES = 4


def fold(block):
    total = None
    for r in range(0, block.shape[0], 8):
        for c in range(0, block.shape[1], 128):
            tile = block[r : r + 8, c : c + 128]
            total = tile if total is None else total + tile
    return total


def kernel(
    chips, groups, chunk, threshold, grads, outer, moment, params_out, moment_out,
    average, local, staged, paired, outgoing, arrived, pair_sums, chip_sums, group_sums, total_sum,
    load_sem, state_sem, pair_send, pair_recv, part_send, part_recv, full_send, full_recv,
    share_send, share_recv, sum_send, sum_recv, ready,
):
    rows, cols = average.shape
    half = rows // CORES
    piece = half // chips
    count = piece // chunk
    island = lax.axis_index("island")
    group = lax.axis_index("fsdp")
    chip, core = lax.div(island, CORES), lax.rem(island, CORES)
    other = 1 - core
    sibling = {"island": chip * CORES + other}

    def owner(p):
        return lax.rem(chip + p, chips)

    def peer(p):
        return {"island": owner(p) * CORES + core}

    def start_of(which_core, p, j):
        return pl.multiple_of(which_core * half + owner(p) * piece + j * chunk, chunk)

    def span(j):
        return pl.ds(pl.multiple_of(j * chunk, chunk), chunk)

    barrier = pltpu.get_barrier_semaphore()
    lead = core == 0
    mates = [{"fsdp": lax.rem(group + s, groups)} for s in range(1, groups)]

    @pl.when(lead)
    def _():
        for p in range(chips):
            pl.semaphore_signal(
                barrier, inc=1, device_id={"island": owner(p) * CORES + 1}, device_id_type=MESH
            )
        for mate in mates:
            pl.semaphore_signal(barrier, inc=1, device_id=mate, device_id_type=MESH)

    @pl.when(jnp.logical_not(lead))
    def _():
        for p in range(1, chips):
            pl.semaphore_signal(barrier, inc=1, device_id=peer(p), device_id_type=MESH)

    def load(side, p):
        which = other if side == 0 else core
        place = pl.ds(start_of(which, p, 0), piece)
        return pltpu.make_async_copy(
            grads.at[0, place], local.at[place], load_sem.at[side, p]
        )

    order = [*range(1, chips), 0]
    for p in order:
        load(0, p).start()
        load(1, p).start()

    state = [
        pltpu.make_async_copy(outer, params_out, state_sem.at[0]),
        pltpu.make_async_copy(moment, moment_out, state_sem.at[1]),
    ]

    def to_sibling(p, j):
        return pltpu.make_async_remote_copy(
            staged.at[p, span(j)], paired.at[p, span(j)],
            pair_send.at[p, j], pair_recv.at[p, j], sibling, MESH,
        )

    def part_to_peer(p, j, back):
        slot = (chips - p if back else p) - 1
        return pltpu.make_async_remote_copy(
            outgoing.at[p - 1, span(j)], arrived.at[slot, span(j)],
            part_send.at[p - 1, j], part_recv.at[slot, j], peer(p), MESH,
        )

    def full_to_peer(p, j, whose, slot):
        place = pl.ds(start_of(core, whose, j), chunk)
        return pltpu.make_async_remote_copy(
            average.at[place], average.at[place],
            full_send.at[p - 1, j], full_recv.at[slot - 1, j], peer(p), MESH,
        )

    def full_to_sibling(p, j, which):
        place = pl.ds(start_of(which, p, j), chunk)
        return pltpu.make_async_remote_copy(
            average.at[place], average.at[place],
            share_send.at[p, j], share_recv.at[p, j], sibling, MESH,
        )

    def each(body):
        lax.fori_loop(0, count, lambda j, _: body(j), None)

    def stage(p, j):
        block = local[pl.ds(start_of(other, p, j), chunk)]
        staged[p, span(j)] = block.astype(jnp.float32)

    def chip_sum(p, j):
        to_sibling(p, j).wait_recv()
        mine = local[pl.ds(start_of(core, p, j), chunk)].astype(jnp.float32)
        return mine + paired[p, span(j)]

    for p in range(1, chips):
        load(0, p).wait()
        each(lambda j, p=p: stage(p, j))
    @pl.when(jnp.logical_not(lead))
    def _():
        pl.semaphore_wait(barrier, chips + (chips - 1))
        pl.semaphore_signal(ready, inc=1, device_id=sibling, device_id_type=MESH)

    @pl.when(lead)
    def _():
        pl.semaphore_wait(ready, 1)

    for p in range(1, chips):
        each(lambda j, p=p: to_sibling(p, j).start())
    for p in range(1, chips):
        load(1, p).wait()

        def send_part(j, p=p):
            outgoing[p - 1, span(j)] = chip_sum(p, j)
            part_to_peer(p, j, True).start()

        each(send_part)
    load(0, 0).wait()

    def send_pair(j):
        stage(0, j)
        to_sibling(0, j).start()

    send_pair(0)
    load(1, 0).wait()
    for copy in state:
        copy.start()

    def gather(j):
        for p in range(1, chips):
            full_to_peer(p, j, 0, chips - p).start()

    def finish(j, partial):
        pl.when(j + 1 < count)(lambda: send_pair(j + 1))
        total = chip_sum(0, j)
        for p in range(1, chips):
            part_to_peer(p, j, False).wait_recv()
            total = total + arrived[p - 1, span(j)]
        mean = total / (chips * CORES)
        average[pl.ds(start_of(core, 0, j), chunk)] = mean
        pl.when(j < AHEAD)(lambda: gather(j))
        full_to_sibling(0, j, core).start()
        return partial + fold(mean * mean)

    partial = lax.fori_loop(0, count, finish, jnp.zeros((8, 128), jnp.float32))

    def sum_copy(slots, mine, number, target):
        return pltpu.make_async_remote_copy(
            slots.at[mine], slots.at[mine],
            sum_send.at[number], sum_recv.at[number], target, MESH,
        )

    def send_sums(slots, mine, value, targets, first):
        slots[mine] = value
        copies = [sum_copy(slots, mine, first + s, t) for s, t in enumerate(targets)]
        for copy in copies:
            copy.start()
        return copies

    def add_up(slots):
        total = slots[0]
        for s in range(1, slots.shape[0]):
            total = total + slots[s]
        return total

    sent = send_sums(chip_sums, chip, partial, [peer(p) for p in range(1, chips)], 2)

    def gather_rest(j, _):
        gather(j)

    lax.fori_loop(min(AHEAD, count), count, gather_rest, None)
    for copy in sent:
        copy.wait_recv()
    pair_sums[core] = add_up(chip_sums)
    from_pair = sum_copy(pair_sums, 1, 0, sibling)
    whole = sum_copy(total_sum, 0, 1, sibling)

    @pl.when(jnp.logical_not(lead))
    def _():
        from_pair.start()
        whole.wait_recv()
        from_pair.wait_send()

    @pl.when(lead)
    def _():
        pl.semaphore_wait(barrier, groups - 1)
        from_pair.wait_recv()
        copies = send_sums(group_sums, group, add_up(pair_sums), mates, 1 + chips)
        for copy in copies:
            copy.wait_recv()
        total_sum[0] = add_up(group_sums)
        whole.start()
        for copy in copies:
            copy.wait_send()
        whole.wait_send()

    squares = jnp.sum(total_sum[0], keepdims=True)
    factor = jnp.minimum(1.0, threshold / jnp.sqrt(squares + 1e-06))
    for copy in state:
        copy.wait()

    def update(which, p, j):
        place = pl.ds(start_of(which, p, j), chunk)
        clipped = factor * average[place]
        moment_next = 0.9 * moment_out[place] + clipped
        moment_out[place] = moment_next
        params_out[place] = params_out[place] - 0.7 * (clipped + 0.9 * moment_next)

    def own(j):
        update(core, 0, j)
        full_to_sibling(0, j, other).wait_recv()
        update(other, 0, j)

    each(own)

    def from_sibling(j):
        for p in range(1, chips):
            full_to_sibling(p, j, other).wait_recv()
            update(other, p, j)

    def forward(j):
        for p in range(1, chips):
            full_to_peer(p, j, p, p).wait_recv()
            full_to_sibling(p, j, core).start()
        for p in range(1, chips):
            update(core, p, j)
        pl.when(j > 0)(lambda: from_sibling(j - 1))

    each(forward)
    from_sibling(count - 1)

    def close(j):
        for p in range(chips):
            full_to_sibling(p, j, core).wait_send()
            to_sibling(p, j).wait_send()
        for p in range(1, chips):
            part_to_peer(p, j, True).wait_send()
            full_to_peer(p, j, 0, p).wait_send()

    each(close)
    for copy in sent:
        copy.wait_send()


def step(islands, groups, grads, outer, moment):
    rows, cols = outer.shape
    chips = islands // CORES
    piece = rows // islands
    chunk = max(16, piece // CHUNKS)
    count = piece // chunk
    threshold = 0.2 * math.sqrt(rows * groups * cols)
    wide = jnp.float32
    dma = pltpu.SemaphoreType.DMA
    return pl.pallas_call(
        functools.partial(kernel, chips, groups, chunk, threshold),
        out_shape=[pltpu.VMEM((rows, cols), wide)] * 2,
        in_specs=[pl.BlockSpec(memory_space=pltpu.HBM)] * 3,
        out_specs=[pl.BlockSpec(memory_space=pltpu.VMEM)] * 2,
        scratch_shapes=[
            pltpu.VMEM((rows, cols), wide),
            pltpu.VMEM((rows, cols), grads.dtype),
            pltpu.VMEM((chips, piece, cols), wide),
            pltpu.VMEM((chips, piece, cols), wide),
            pltpu.VMEM((max(chips - 1, 1), piece, cols), wide),
            pltpu.VMEM((max(chips - 1, 1), piece, cols), wide),
            pltpu.VMEM((CORES, 8, 128), wide),
            pltpu.VMEM((chips, 8, 128), wide),
            pltpu.VMEM((groups, 8, 128), wide),
            pltpu.VMEM((1, 8, 128), wide),
            dma((2, chips)),
            dma((2,)),
            dma((chips, count)),
            dma((chips, count)),
            dma((chips - 1, count)),
            dma((chips - 1, count)),
            dma((chips - 1, count)),
            dma((chips - 1, count)),
            dma((chips, count)),
            dma((chips, count)),
            dma((chips + groups,)),
            dma((chips + groups,)),
            pltpu.SemaphoreType.REGULAR,
        ],
        compiler_params=pltpu.CompilerParams(
            collective_id=0, has_side_effects=True, vmem_limit_bytes=32 * 2**20
        ),
        cost_estimate=pl.CostEstimate(
            flops=16 * rows * cols, bytes_accessed=10 * rows * cols, transcendentals=0
        ),
    )(*(pltpu.with_memory_space_constraint(x, pltpu.HBM) for x in (grads, outer, moment)))


def store_kernel(params, moment, params_out, moment_out, sem):
    part = params.shape[0] // STORES
    copies = []
    for s in range(STORES):
        place = pl.ds(s * part, part)
        for a, (source, target) in enumerate([(params, params_out), (moment, moment_out)]):
            copies.append(pltpu.make_async_copy(source.at[place], target.at[place], sem.at[a, s]))
    for copy in copies:
        copy.start()
    for copy in copies:
        copy.wait()


def store(results):
    return pl.pallas_call(
        store_kernel,
        out_shape=[jax.ShapeDtypeStruct(x.shape, x.dtype) for x in results],
        in_specs=[pl.BlockSpec(memory_space=pltpu.VMEM)] * 2,
        out_specs=[pl.BlockSpec(memory_space=pltpu.HBM)] * 2,
        scratch_shapes=[pltpu.SemaphoreType.DMA((2, STORES))],
        compiler_params=pltpu.CompilerParams(vmem_limit_bytes=4 * 2**20),
    )(*(pltpu.with_memory_space_constraint(x, pltpu.VMEM) for x in results))


def per_device(pseudo_grads, outer_params, momentum):
    islands, groups = lax.axis_size("island"), lax.axis_size("fsdp")
    return tuple(store(step(islands, groups, pseudo_grads, outer_params, momentum)))


def solution(mesh):
    return jax.shard_map(
        per_device,
        mesh=mesh,
        in_specs=(P("island", "fsdp", None), P("fsdp", None), P("fsdp", None)),
        out_specs=(P("fsdp", None), P("fsdp", None)),
        check_vma=False,
    )
```
